32 devices in a mesh: groups: 2 (over x), blocks: 16 (over z, y, core).
Axes of the slice: x: 2, y: 2, z: 4, core: 2. Of those that a mesh axis runs over, the one named last changes fastest.
Arguments:
- query: bfloat16 [16384, 1024], P(('groups', 'blocks')), parts along dimension 0, may hold values from -90 to 90
- keys: bfloat16 [16384, 128], P(('groups', 'blocks')), parts along dimension 0, may hold values from -4.5 to 4.5
- values: bfloat16 [16384, 128], P(('groups', 'blocks')), parts along dimension 0, may hold values from -5 to 5
- out_attn: bfloat16 [16384, 1024], P(('groups', 'blocks')), parts along dimension 0, may hold values from -1.5 to 1.5
- dout: bfloat16 [16384, 1024], P(('groups', 'blocks')), parts along dimension 0, may hold values from -6 to 6
- docs: int32 [16384], P(('groups', 'blocks')), parts along dimension 0, may hold values from 0 to 9, never falling along the last dimension, each value on 1 to 1537 neighbouring positions
Outputs:
- dquery: bfloat16 [16384, 1024], P(('groups', 'blocks')), parts along dimension 0
- dkeys: bfloat16 [16384, 128], P(('groups', 'blocks')), parts along dimension 0
- dvalues: bfloat16 [16384, 128], P(('groups', 'blocks')), parts along dimension 0
The draws below stay inside these ranges and needn't reach their ends.
There are 2 independent parts, one for each index of `groups`. The reference program is written for one: setup_inputs(seed, part) draws one part's arguments, and reference() takes and returns one part's arrays. A program takes and returns all parts, laid end to end along the dimension named above; each array names one. Nothing has to cross between parts.
Inputs may be any that keep to these rules, and one draw needn't show every extreme that they name: `docs`: document numbers never fall along the tokens and start at 0; each document has 1 to 1537 tokens, and one has exactly 1537.
All inputs are finite; a program needn't handle non-finite values.
Results may differ from the reference program's by a relative error of at most 0.0052.
Values may be sent and summed in bfloat16 or wider, within the bound.
A program may use at most 64 MiB of HBM per device.

```python
import math
import jax
import jax.numpy as jnp
import numpy as np
from jax import lax

HEADS = 8
HD = 128
BLOCK = 512
REACH = 3
TOKENS = 8192
DOCS = 10
DOC_MOST = 1537


def paired_draw(key):
    key_seed = jax.random.fold_in(key, 101)
    query_seed = jax.random.fold_in(key, 102)
    key_rows = jnp.clip(jax.random.normal(key_seed, (TOKENS, HD), jnp.float32), -4.0, 4.0)
    query_rows = jnp.clip(jax.random.normal(query_seed, (TOKENS, HEADS, HD), jnp.float32), -4.0, 4.0)
    return (query_rows, key_rows)


def draw_query(key, part):
    query_rows, key_rows = paired_draw(key)
    return query_rows.reshape(TOKENS, HEADS * HD).astype(jnp.bfloat16)


def draw_keys(key, part):
    query_rows, key_rows = paired_draw(key)
    return key_rows.astype(jnp.bfloat16)


def block_levels(own_key, dims, split, low, top_value):
    gain = 1.0
    for position, shards_of in split:
        steps = jax.random.uniform(jax.random.fold_in(jax.random.fold_in(own_key, 6), position), (shards_of,), jnp.float32, low / len(split), top_value / len(split))
        gain = gain * jnp.repeat(jnp.exp(steps), dims[position] // shards_of).reshape((-1,) + (1,) * (len(dims) - 1 - position))
    return gain


def split_up(number_of, total, reach, lean):
    loads = [(1 << 20) // math.isqrt(standing ** lean) + 1 for standing in range(2, number_of + 1)]
    rest, counts = total - reach - (number_of - 1), [1] * (number_of - 1)
    while rest > 0:
        candidates = [i for i in range(number_of - 1) if counts[i] < reach]
        pool, remaining = sum([loads[i] for i in candidates]), rest
        for i in candidates:
            more = min(reach - counts[i], max(1, remaining * loads[i] // pool), rest)
            counts[i] = counts[i] + more
            rest = rest - more
    return np.array([reach] + counts)


def ragged(key, number_of, total, bound, skew):
    if number_of == 2:
        one = jax.random.randint(key, (), max(1, total - bound), min(bound, total - 1) + 1)
        return jnp.stack([one, total - one])
    tallies = jnp.asarray(split_up(number_of, total, bound, skew), jnp.int32)
    twos = (number_of - 1) // 2
    source_of, sink = tallies[1:1 + 2 * twos:2], tallies[2:2 + 2 * twos:2]
    slack = jnp.minimum(source_of - 1, bound - sink)
    moved = jax.random.randint(jax.random.fold_in(key, 1), (twos,), 0, 1 << 20) % (slack + 1)
    tallies = tallies.at[1:1 + 2 * twos:2].set(source_of - moved).at[2:2 + 2 * twos:2].set(sink + moved)
    return tallies[jax.random.permutation(jax.random.fold_in(key, 2), number_of)]


def bell_draw(key, extent, scale, most, split=(), kind=jnp.bfloat16):
    entries = jax.random.normal(key, extent, jnp.float32) * scale
    if len(split) > 0:
        entries = block_levels(key, extent, split, -0.22, 0.18) * entries
    return jnp.clip(entries, min=-most, max=most).astype(kind)


def setup_inputs(seed: int = 0, part: int = 0) -> dict:
    arg_keys = jax.random.split(jax.random.key(seed), 7)
    part_keys = jax.random.split(jax.random.fold_in(arg_keys[6], part), 7)
    query = draw_query(jax.random.fold_in(jax.random.fold_in(arg_keys[6], part), 71), part)
    keys = draw_keys(jax.random.fold_in(jax.random.fold_in(arg_keys[6], part), 71), part)
    values = bell_draw(part_keys[2], (TOKENS, HD), 1.0, 5.0, ((0, 16),))
    out_attn = bell_draw(part_keys[3], (TOKENS, HEADS * HD), 0.25, 1.5, ((0, 16),))
    dout = bell_draw(part_keys[4], (TOKENS, HEADS * HD), 1.0, 6.0, ((0, 16),))
    docs = jnp.searchsorted(jnp.cumsum(ragged(part_keys[5], DOCS, TOKENS, DOC_MOST, 1)), jnp.arange(TOKENS), side="right").astype(jnp.int32)
    return {"query": query, "keys": keys, "values": values, "out_attn": out_attn, "dout": dout, "docs": docs}


def reference(query, keys, values, out_attn, dout, docs):
    token_count = keys.shape[0]
    key_span = REACH + 1
    front_pad = REACH * BLOCK
    score_scale = 1.0 / math.sqrt(HD)
    positions = jnp.arange(token_count, dtype=jnp.int32)
    previous = jnp.concatenate([docs[:1], docs[:-1]])
    boundary = jnp.where(docs != previous, positions, 0).astype(jnp.int32)
    doc_start = lax.cummax(boundary, axis=0)
    key_pad = jnp.concatenate([jnp.zeros((front_pad, HD), keys.dtype), keys], axis=0)
    value_pad = jnp.concatenate([jnp.zeros((front_pad, HD), values.dtype), values], axis=0)

    def one_block(totals, block_id):
        first_row = (block_id * BLOCK).astype(jnp.int32)
        query_rows = lax.dynamic_slice_in_dim(query, first_row, BLOCK, 0).reshape(BLOCK * HEADS, HD).astype(jnp.float32)
        dout_rows = lax.dynamic_slice_in_dim(dout, first_row, BLOCK, 0).reshape(BLOCK * HEADS, HD).astype(jnp.float32)
        out_rows = lax.dynamic_slice_in_dim(out_attn, first_row, BLOCK, 0).reshape(BLOCK * HEADS, HD).astype(jnp.float32)
        key_part = lax.dynamic_slice_in_dim(key_pad, first_row, key_span * BLOCK, 0).astype(jnp.float32)
        value_part = lax.dynamic_slice_in_dim(value_pad, first_row, key_span * BLOCK, 0).astype(jnp.float32)
        start_rows = lax.dynamic_slice_in_dim(doc_start, first_row, BLOCK, 0)
        pos_rows = first_row + jnp.arange(BLOCK, dtype=jnp.int32)
        key_pos = first_row - front_pad + jnp.arange(key_span * BLOCK, dtype=jnp.int32)
        visible = (key_pos[None, :] >= start_rows[:, None]) & (key_pos[None, :] <= pos_rows[:, None])
        scores = jnp.dot(query_rows, key_part.T, preferred_element_type=jnp.float32) * score_scale
        scores = scores.reshape(BLOCK, HEADS, key_span * BLOCK)
        masked = jnp.where(visible[:, None, :], scores, -1e+30)
        row_max = lax.optimization_barrier(jnp.max(masked, axis=-1, keepdims=True))
        log_total = row_max + jnp.log(lax.optimization_barrier(jnp.sum(jnp.exp(masked - row_max), axis=-1, keepdims=True)))
        prob_full = jnp.where(visible[:, None, :], jnp.exp(masked - log_total), 0.0)
        prob_full = prob_full.reshape(BLOCK * HEADS, key_span * BLOCK)
        prob_half = lax.optimization_barrier(prob_full.astype(jnp.bfloat16)).astype(jnp.float32)
        delta_rows = lax.optimization_barrier(jnp.sum(dout_rows * out_rows, axis=-1))
        grad_prob = jnp.dot(dout_rows, value_part.T, preferred_element_type=jnp.float32)
        grad_score = prob_full * (grad_prob - delta_rows[:, None])
        score_half = lax.optimization_barrier(grad_score.astype(jnp.bfloat16)).astype(jnp.float32)
        grad_query = (score_scale * jnp.dot(score_half, key_part, preferred_element_type=jnp.float32)).astype(jnp.bfloat16)
        key_grad = score_scale * jnp.dot(score_half.T, query_rows, preferred_element_type=jnp.float32)
        value_grad = jnp.dot(prob_half.T, dout_rows, preferred_element_type=jnp.float32)
        old_key = lax.dynamic_slice_in_dim(totals[0], first_row, key_span * BLOCK, 0)
        old_value = lax.dynamic_slice_in_dim(totals[1], first_row, key_span * BLOCK, 0)
        new_key = lax.dynamic_update_slice_in_dim(totals[0], old_key + key_grad, first_row, 0)
        new_value = lax.dynamic_update_slice_in_dim(totals[1], old_value + value_grad, first_row, 0)
        return ((new_key, new_value), grad_query.reshape(BLOCK, HEADS * HD))
    start_totals = (jnp.zeros((token_count + front_pad, HD), jnp.float32), jnp.zeros((token_count + front_pad, HD), jnp.float32))
    block_ids = jnp.arange(token_count // BLOCK, dtype=jnp.int32)
    totals, grad_blocks = lax.scan(one_block, start_totals, block_ids)
    dquery = grad_blocks.reshape(token_count, HEADS * HD)
    dkeys = totals[0][front_pad:].astype(jnp.bfloat16)
    dvalues = totals[1][front_pad:].astype(jnp.bfloat16)
    return (dquery, dkeys, dvalues)
```

```python
import functools
import math

import jax
import jax.numpy as jnp
from jax import lax
from jax.experimental import pallas as pl
from jax.experimental.pallas import tpu as pltpu
from jax.sharding import PartitionSpec as P

REACH = 3
FAR = 2.0**18
MESH = pl.DeviceIdType.MESH
NT = (((1,), (1,)), ((), ()))


def greet_and_count(sources, waits, count):
    barrier = pltpu.get_barrier_semaphore()
    for other in sources:

        @pl.when((other >= 0) & (other < count))
        def _():
            pl.semaphore_signal(
                barrier, inc=1, device_id={"blocks": other}, device_id_type=MESH
            )

    @pl.when(waits > 0)
    def _():
        pl.semaphore_wait(barrier, waits)


def gather_kernel(
    count, k_ref, v_ref, d_ref, kaug_ref, vall_ref, docs_ref,
    k_in, v_in, d_out, d_in, send_sem, recv_sem,
):
    me = lax.axis_index("blocks")
    rows = k_ref.shape[0]
    width = k_ref.shape[1]
    d_out[...] = jnp.broadcast_to(d_ref[...], d_out.shape)
    greet_and_count(
        [me - step for step in range(1, REACH + 1)],
        jnp.minimum(count - 1 - me, REACH),
        count,
    )

    def copies(step):
        slot = REACH - step
        pairs = ((k_ref, k_in), (v_ref, v_in), (d_out, d_in))
        return [
            pltpu.make_async_remote_copy(
                src_ref=src,
                dst_ref=dst.at[slot],
                send_sem=send_sem.at[slot, i],
                recv_sem=recv_sem.at[slot, i],
                device_id={"blocks": me + step},
                device_id_type=MESH,
            )
            for i, (src, dst) in enumerate(pairs)
        ]

    for step in range(REACH, 0, -1):

        @pl.when(me + step < count)
        def _():
            for copy in copies(step):
                copy.start()

    def place(block, k_rows, v_rows, doc_row):
        hot = lax.broadcasted_iota(jnp.int32, (width, rows), 0) == doc_row
        feature = jnp.transpose(jnp.where(hot, 0.0, -FAR).astype(jnp.float32))
        kaug_ref[pl.ds(block * rows, rows), :width] = k_rows
        kaug_ref[pl.ds(block * rows, rows), width:] = feature.astype(jnp.bfloat16)
        vall_ref[pl.ds(block * rows, rows), :] = v_rows
        docs_ref[block : block + 1, :] = doc_row

    place(REACH, k_ref[...], v_ref[...], d_ref[...])
    for step in range(1, REACH + 1):
        slot = REACH - step

        @pl.when(me - step >= 0)
        def _():
            for copy in copies(step):
                copy.wait_recv()
            place(slot, k_in[slot], v_in[slot], d_in[slot, :1, :])

        @pl.when(me - step < 0)
        def _():
            zero = jnp.zeros((rows, width), jnp.bfloat16)
            place(slot, zero, zero, jnp.full((1, rows), -1, jnp.int32))

    for step in range(1, REACH + 1):

        @pl.when(me + step < count)
        def _():
            for copy in copies(step):
                copy.wait_send()


def attend_kernel(
    heads, tile,
    q_ref, o_ref, g_ref, kaug_ref, v_ref, docs_ref,
    dq_ref, part_ref, own_ref,
    s_scr, p_scr, ds_scr, kt_scr, dqt_scr, qa_scr, qs_scr, gs_scr, dk_scr, dv_scr,
):
    rows = q_ref.shape[0]
    width = v_ref.shape[1]
    window = v_ref.shape[0]
    scale = 1.0 / math.sqrt(width)
    to_two = scale * math.log2(math.e)
    past = window - rows
    dk_scr[...] = jnp.zeros_like(dk_scr)
    dv_scr[...] = jnp.zeros_like(dv_scr)
    for low in range(0, window, tile):
        kt_scr[:, low : low + tile] = jnp.transpose(
            kaug_ref[low : low + tile, :width].astype(jnp.float32)
        ).astype(jnp.bfloat16)
    ones = jnp.ones((8, 2 * width), jnp.bfloat16)
    docs = docs_ref[...]
    tri = jnp.where(
        lax.broadcasted_iota(jnp.int32, (tile, tile), 0)
        <= lax.broadcasted_iota(jnp.int32, (tile, tile), 1),
        0.0,
        -FAR,
    ).astype(jnp.float32)

    for j in range(rows // tile):
        own = slice(j * tile, (j + 1) * tile)
        doc_first = docs_ref[REACH : REACH + 1, j * tile : j * tile + 1]
        before = jnp.sum(jnp.where(docs < doc_first, 1.0, 0.0)).astype(jnp.int32)
        first = before // tile
        last = past // tile + j
        hot = jnp.where(kaug_ref[past + j * tile : past + (j + 1) * tile, width:] == 0, 1.0, 0.0)
        hot = hot.astype(jnp.bfloat16)
        deltas = []
        for h in range(heads):
            cols = slice(h * width, (h + 1) * width)
            qh = q_ref[own, cols]
            gh = g_ref[own, cols]
            qa_scr[h, :, :width] = qh
            qa_scr[h, :, width:] = hot
            qs_scr[h * tile : (h + 1) * tile, :] = qh
            gs_scr[h * tile : (h + 1) * tile, :] = gh
            both = gh.astype(jnp.float32) * o_ref[own, cols].astype(jnp.float32)
            high = both.astype(jnp.bfloat16)
            less = (both - high.astype(jnp.float32)).astype(jnp.bfloat16)
            deltas.append(
                lax.dot_general(
                    ones, jnp.concatenate([high, less], axis=1), NT,
                    preferred_element_type=jnp.float32,
                )[:1]
            )

        def fold(part, how):
            return how(part.reshape(tile // 8, 8, tile), axis=0)

        def score(c, tops, bias):
            at = pl.ds(pl.multiple_of(c * tile, tile), tile)
            kc = kaug_ref[at, :]
            new = []
            for h in range(heads):
                s = lax.dot_general(kc, qa_scr[h], NT, preferred_element_type=jnp.float32)
                if bias is not None:
                    s = s + bias
                s_scr[h, at, :] = s
                new.append(jnp.maximum(tops[h], fold(s, jnp.max)))
            return tuple(new)

        tops = tuple(jnp.full((8, tile), -1e30, jnp.float32) for _ in range(heads))
        tops = lax.fori_loop(first, last, lambda c, t: score(c, t, None), tops)
        tops = score(last, tops, tri)
        tops = [jnp.max(t, axis=0, keepdims=True) for t in tops]

        def expo(c, sums):
            at = pl.ds(pl.multiple_of(c * tile, tile), tile)
            new = []
            for h in range(heads):
                e = jnp.exp2((s_scr[h, at, :] - tops[h]) * to_two)
                s_scr[h, at, :] = e
                new.append(sums[h] + fold(e, jnp.sum))
            return tuple(new)

        sums = tuple(jnp.zeros((8, tile), jnp.float32) for _ in range(heads))
        sums = lax.fori_loop(first, last + 1, expo, sums)
        shares = [1.0 / jnp.sum(t, axis=0, keepdims=True) for t in sums]
        dqt_scr[...] = jnp.zeros_like(dqt_scr)

        def grads(c, carry):
            at = pl.ds(pl.multiple_of(c * tile, tile), tile)
            vc = v_ref[at, :]
            kt = kt_scr[:, at]
            for h in range(heads):
                here = slice(h * tile, (h + 1) * tile)
                gp = lax.dot_general(
                    vc, gs_scr[here, :], NT, preferred_element_type=jnp.float32
                )
                p = s_scr[h, at, :] * shares[h]
                p_scr[:, here] = p.astype(jnp.bfloat16)
                ds = (p * (gp - deltas[h])).astype(jnp.bfloat16)
                ds_scr[:, here] = ds
                dqt_scr[h] += jnp.dot(kt, ds, preferred_element_type=jnp.float32)
            dv_scr[at, :] += jnp.dot(
                p_scr[...], gs_scr[...], preferred_element_type=jnp.float32
            )
            dk_scr[at, :] += jnp.dot(
                ds_scr[...], qs_scr[...], preferred_element_type=jnp.float32
            )
            return carry

        lax.fori_loop(first, last + 1, grads, 0)
        for h in range(heads):
            dq_ref[own, h * width : (h + 1) * width] = jnp.transpose(
                dqt_scr[h] * scale
            ).astype(jnp.bfloat16)

    part_ref[:, :width] = (dk_scr[:past, :] * scale).astype(jnp.bfloat16)
    part_ref[:, width:] = dv_scr[:past, :].astype(jnp.bfloat16)
    own_ref[:, :width] = dk_scr[past:, :] * scale
    own_ref[:, width:] = dv_scr[past:, :]


def return_kernel(count, part_ref, own_ref, dk_ref, dv_ref, held, send_sem, recv_sem):
    me = lax.axis_index("blocks")
    rows, width = dk_ref.shape
    greet_and_count(
        [me + step for step in range(1, REACH + 1)],
        jnp.minimum(me, REACH),
        count,
    )

    def copy(step):
        slot = REACH - step
        return pltpu.make_async_remote_copy(
            src_ref=part_ref.at[pl.ds(slot * rows, rows), :],
            dst_ref=held.at[slot],
            send_sem=send_sem.at[slot],
            recv_sem=recv_sem.at[slot],
            device_id={"blocks": me - step},
            device_id_type=MESH,
        )

    for step in range(REACH, 0, -1):

        @pl.when(me - step >= 0)
        def _():
            copy(step).start()

        @pl.when(me + step >= count)
        def _():
            held[REACH - step] = jnp.zeros(held.shape[1:], held.dtype)

    for step in range(1, REACH + 1):

        @pl.when(me + step < count)
        def _():
            copy(step).wait_recv()

    total = own_ref[...]
    for step in range(1, REACH + 1):
        total = total + held[REACH - step].astype(jnp.float32)
    dk_ref[...] = total[:, :width].astype(jnp.bfloat16)
    dv_ref[...] = total[:, width:].astype(jnp.bfloat16)
    for step in range(1, REACH + 1):

        @pl.when(me - step >= 0)
        def _():
            copy(step).wait_send()


def local(count, query, keys, values, out_attn, dout, docs):
    rows, width = keys.shape
    heads = query.shape[1] // width
    window = (REACH + 1) * rows
    tile = math.gcd(rows, 256)
    bf16, f32 = jnp.bfloat16, jnp.float32
    vmem = pl.BlockSpec(memory_space=pltpu.VMEM)
    shape = jax.ShapeDtypeStruct
    kaug, v_all, doc_all = pl.pallas_call(
        functools.partial(gather_kernel, count),
        out_shape=(
            shape((window, 2 * width), bf16),
            shape((window, width), bf16),
            shape((REACH + 1, rows), jnp.int32),
        ),
        in_specs=[vmem] * 3,
        out_specs=(vmem,) * 3,
        scratch_shapes=[
            pltpu.VMEM((REACH, rows, width), bf16),
            pltpu.VMEM((REACH, rows, width), bf16),
            pltpu.VMEM((8, rows), jnp.int32),
            pltpu.VMEM((REACH, 8, rows), jnp.int32),
            pltpu.SemaphoreType.DMA((REACH, 3)),
            pltpu.SemaphoreType.DMA((REACH, 3)),
        ],
        compiler_params=pltpu.CompilerParams(
            collective_id=0, has_side_effects=True, vmem_limit_bytes=16 << 20
        ),
    )(keys, values, docs.reshape(1, rows))
    dquery, part, own = pl.pallas_call(
        functools.partial(attend_kernel, heads, tile),
        out_shape=(
            shape(query.shape, bf16),
            shape((window - rows, 2 * width), bf16),
            shape((rows, 2 * width), f32),
        ),
        in_specs=[vmem] * 6,
        out_specs=(vmem,) * 3,
        scratch_shapes=[
            pltpu.VMEM((heads, window, tile), f32),
            pltpu.VMEM((tile, heads * tile), bf16),
            pltpu.VMEM((tile, heads * tile), bf16),
            pltpu.VMEM((width, window), bf16),
            pltpu.VMEM((heads, width, tile), f32),
            pltpu.VMEM((heads, tile, 2 * width), bf16),
            pltpu.VMEM((heads * tile, width), bf16),
            pltpu.VMEM((heads * tile, width), bf16),
            pltpu.VMEM((window, width), f32),
            pltpu.VMEM((window, width), f32),
        ],
        compiler_params=pltpu.CompilerParams(vmem_limit_bytes=48 << 20),
    )(query, out_attn, dout, kaug, v_all, doc_all)
    dkeys, dvalues = pl.pallas_call(
        functools.partial(return_kernel, count),
        out_shape=(shape((rows, width), bf16), shape((rows, width), bf16)),
        in_specs=[vmem] * 2,
        out_specs=(vmem,) * 2,
        scratch_shapes=[
            pltpu.VMEM((REACH, rows, 2 * width), bf16),
            pltpu.SemaphoreType.DMA((REACH,)),
            pltpu.SemaphoreType.DMA((REACH,)),
        ],
        compiler_params=pltpu.CompilerParams(
            collective_id=1, has_side_effects=True, vmem_limit_bytes=16 << 20
        ),
    )(part, own)
    return (dquery, dkeys, dvalues)


def solution(mesh):
    rows = P(("groups", "blocks"), None)
    return jax.shard_map(
        functools.partial(local, mesh.shape["blocks"]),
        mesh=mesh,
        in_specs=(rows,) * 5 + (P(("groups", "blocks")),),
        out_specs=(rows,) * 3,
        check_vma=False,
    )
```

```python
import functools
import math

import jax
import jax.numpy as jnp
from jax import lax
from jax.experimental import pallas as pl
from jax.experimental.pallas import tpu as pltpu
from jax.sharding import PartitionSpec as P

REACH = 3
FAR = 2.0**18
MESH = pl.DeviceIdType.MESH
NT = (((1,), (1,)), ((), ()))


def greet_and_count(sources, waits, count):
    barrier = pltpu.get_barrier_semaphore()
    for other in sources:

        @pl.when((other >= 0) & (other < count))
        def _():
            pl.semaphore_signal(
                barrier, inc=1, device_id={"blocks": other}, device_id_type=MESH
            )

    @pl.when(waits > 0)
    def _():
        pl.semaphore_wait(barrier, waits)


def gather_kernel(
    count, k_ref, v_ref, d_ref, kaug_ref, kt_ref, vall_ref, docs_ref,
    k_in, v_in, d_out, d_in, send_sem, recv_sem, own_sem,
):
    me = lax.axis_index("blocks")
    rows = k_ref.shape[0]
    width = k_ref.shape[1]
    bring = [
        pltpu.make_async_copy(src, dst.at[REACH], own_sem.at[i])
        for i, (src, dst) in enumerate(((k_ref, k_in), (v_ref, v_in)))
    ]
    for copy in bring:
        copy.start()
    d_out[...] = jnp.broadcast_to(d_ref[...], d_out.shape)
    greet_and_count(
        [me - step for step in range(1, REACH + 1)],
        jnp.minimum(count - 1 - me, REACH),
        count,
    )

    def copies(step):
        slot = REACH - step
        pairs = ((k_ref, k_in), (v_ref, v_in), (d_out, d_in))
        return [
            pltpu.make_async_remote_copy(
                src_ref=src,
                dst_ref=dst.at[slot],
                send_sem=send_sem.at[slot, i],
                recv_sem=recv_sem.at[slot, i],
                device_id={"blocks": me + step},
                device_id_type=MESH,
            )
            for i, (src, dst) in enumerate(pairs)
        ]

    for step in range(REACH, 0, -1):

        @pl.when(me + step < count)
        def _():
            for copy in copies(step):
                copy.start()

    def place(block, k_rows, v_rows, doc_row):
        hot = lax.broadcasted_iota(jnp.int32, (width, rows), 0) == doc_row
        feature = jnp.transpose(jnp.where(hot, 0.0, -FAR).astype(jnp.float32))
        kaug_ref[pl.ds(block * rows, rows), :width] = k_rows
        kaug_ref[pl.ds(block * rows, rows), width:] = feature.astype(jnp.bfloat16)
        kt_ref[:, pl.ds(block * rows, rows)] = jnp.transpose(k_rows)
        vall_ref[pl.ds(block * rows, rows), :] = v_rows
        docs_ref[block : block + 1, :] = doc_row

    for copy in bring:
        copy.wait()
    place(REACH, k_in[REACH], v_in[REACH], d_ref[...])
    for step in range(1, REACH + 1):
        slot = REACH - step

        @pl.when(me - step >= 0)
        def _():
            for copy in copies(step):
                copy.wait_recv()
            place(slot, k_in[slot], v_in[slot], d_in[slot, :1, :])

        @pl.when(me - step < 0)
        def _():
            zero = jnp.zeros((rows, width), jnp.bfloat16)
            place(slot, zero, zero, jnp.full((1, rows), -1, jnp.int32))

    for step in range(1, REACH + 1):

        @pl.when(me + step < count)
        def _():
            for copy in copies(step):
                copy.wait_send()


def attend_kernel(
    heads, tile,
    q_hbm, o_hbm, g_hbm, kaug_ref, kt_ref, v_ref, docs_ref,
    dq_ref, part_ref, own_ref,
    q_ref, o_ref, g_ref,
    s_scr, p_scr, ds_scr, dqt_scr, qa_scr, gt_scr, qs_scr, gs_scr, dk_scr, dv_scr, sems,
):
    rows = q_ref.shape[0]
    width = v_ref.shape[1]
    window = v_ref.shape[0]
    scale = 1.0 / math.sqrt(width)
    to_two = scale * math.log2(math.e)
    past = window - rows

    def bring(j):
        part = pl.ds(j * tile, tile)
        pairs = ((q_hbm, q_ref), (g_hbm, g_ref), (o_hbm, o_ref))
        return [
            pltpu.make_async_copy(src.at[part, :], dst.at[part, :], sems.at[j, i])
            for i, (src, dst) in enumerate(pairs)
        ]

    for j in range(rows // tile):
        for copy in bring(j):
            copy.start()
    dk_scr[...] = jnp.zeros_like(dk_scr)
    dv_scr[...] = jnp.zeros_like(dv_scr)
    ones = jnp.ones((8, 2 * width), jnp.bfloat16)
    docs = docs_ref[...]
    tri = jnp.where(
        lax.broadcasted_iota(jnp.int32, (tile, tile), 0)
        <= lax.broadcasted_iota(jnp.int32, (tile, tile), 1),
        0.0,
        -FAR,
    ).astype(jnp.float32)

    for j in range(rows // tile):
        own = slice(j * tile, (j + 1) * tile)
        doc_first = docs_ref[REACH : REACH + 1, j * tile : j * tile + 1]
        before = jnp.sum(jnp.where(docs < doc_first, 1.0, 0.0)).astype(jnp.int32)
        first = before // tile
        last = past // tile + j
        hot = lax.broadcasted_iota(jnp.int32, (width, tile), 0) == docs[REACH:, own]
        hot = jnp.where(hot, 1.0, 0.0).astype(jnp.bfloat16)
        for copy in bring(j):
            copy.wait()
        deltas = []
        for h in range(heads):
            cols = slice(h * width, (h + 1) * width)
            qh = q_ref[own, cols]
            gh = g_ref[own, cols]
            qa_scr[h, :width, :] = jnp.transpose(qh)
            qa_scr[h, width:, :] = hot
            gt_scr[h] = jnp.transpose(gh)
            qs_scr[h * tile : (h + 1) * tile, :] = qh
            gs_scr[h * tile : (h + 1) * tile, :] = gh
            both = gh.astype(jnp.float32) * o_ref[own, cols].astype(jnp.float32)
            high = both.astype(jnp.bfloat16)
            less = (both - high.astype(jnp.float32)).astype(jnp.bfloat16)
            deltas.append(
                lax.dot_general(
                    ones, jnp.concatenate([high, less], axis=1), NT,
                    preferred_element_type=jnp.float32,
                )[:1]
            )

        def fold(part, how):
            return how(part.reshape(tile // 8, 8, tile), axis=0)

        def score(c, tops, bias):
            at = pl.ds(pl.multiple_of(c * tile, tile), tile)
            kc = kaug_ref[at, :]
            new = []
            for h in range(heads):
                s = jnp.dot(kc, qa_scr[h], preferred_element_type=jnp.float32)
                if bias is not None:
                    s = s + bias
                s_scr[h, at, :] = s
                new.append(jnp.maximum(tops[h], fold(s, jnp.max)))
            return tuple(new)

        tops = tuple(jnp.full((8, tile), -1e30, jnp.float32) for _ in range(heads))
        tops = lax.fori_loop(first, last, lambda c, t: score(c, t, None), tops)
        tops = score(last, tops, tri)
        tops = [jnp.max(t, axis=0, keepdims=True) for t in tops]

        def expo(c, sums):
            at = pl.ds(pl.multiple_of(c * tile, tile), tile)
            new = []
            for h in range(heads):
                e = jnp.exp2((s_scr[h, at, :] - tops[h]) * to_two)
                s_scr[h, at, :] = e
                new.append(sums[h] + fold(e, jnp.sum))
            return tuple(new)

        sums = tuple(jnp.zeros((8, tile), jnp.float32) for _ in range(heads))
        sums = lax.fori_loop(first, last + 1, expo, sums)
        shares = [1.0 / jnp.sum(t, axis=0, keepdims=True) for t in sums]
        dqt_scr[...] = jnp.zeros_like(dqt_scr)

        def grads(c, carry):
            at = pl.ds(pl.multiple_of(c * tile, tile), tile)
            vc = v_ref[at, :]
            kt = kt_ref[:, at]
            for h in range(heads):
                here = slice(h * tile, (h + 1) * tile)
                gp = jnp.dot(vc, gt_scr[h], preferred_element_type=jnp.float32)
                p = s_scr[h, at, :] * shares[h]
                p_scr[:, here] = p.astype(jnp.bfloat16)
                ds = (p * (gp - deltas[h])).astype(jnp.bfloat16)
                ds_scr[:, here] = ds
                dqt_scr[h] += jnp.dot(kt, ds, preferred_element_type=jnp.float32)
            dv_scr[at, :] += jnp.dot(
                p_scr[...], gs_scr[...], preferred_element_type=jnp.float32
            )
            dk_scr[at, :] += jnp.dot(
                ds_scr[...], qs_scr[...], preferred_element_type=jnp.float32
            )
            return carry

        lax.fori_loop(first, last + 1, grads, 0)
        for h in range(heads):
            dq_ref[own, h * width : (h + 1) * width] = jnp.transpose(
                dqt_scr[h] * scale
            ).astype(jnp.bfloat16)

    part_ref[:, :width] = (dk_scr[:past, :] * scale).astype(jnp.bfloat16)
    part_ref[:, width:] = dv_scr[:past, :].astype(jnp.bfloat16)
    own_ref[:, :width] = dk_scr[past:, :] * scale
    own_ref[:, width:] = dv_scr[past:, :]


def return_kernel(
    count, part_ref, own_hbm, dk_ref, dv_ref, held, own_ref, send_sem, recv_sem, own_sem
):
    me = lax.axis_index("blocks")
    bring = pltpu.make_async_copy(own_hbm, own_ref, own_sem)
    bring.start()
    rows, width = dk_ref.shape
    greet_and_count(
        [me + step for step in range(1, REACH + 1)],
        jnp.minimum(me, REACH),
        count,
    )

    def copy(step):
        slot = REACH - step
        return pltpu.make_async_remote_copy(
            src_ref=part_ref.at[pl.ds(slot * rows, rows), :],
            dst_ref=held.at[slot],
            send_sem=send_sem.at[slot],
            recv_sem=recv_sem.at[slot],
            device_id={"blocks": me - step},
            device_id_type=MESH,
        )

    for step in range(REACH, 0, -1):

        @pl.when(me - step >= 0)
        def _():
            copy(step).start()

        @pl.when(me + step >= count)
        def _():
            held[REACH - step] = jnp.zeros(held.shape[1:], held.dtype)

    for step in range(1, REACH + 1):

        @pl.when(me + step < count)
        def _():
            copy(step).wait_recv()

    bring.wait()
    total = own_ref[...]
    for step in range(1, REACH + 1):
        total = total + held[REACH - step].astype(jnp.float32)
    dk_ref[...] = total[:, :width].astype(jnp.bfloat16)
    dv_ref[...] = total[:, width:].astype(jnp.bfloat16)
    for step in range(1, REACH + 1):

        @pl.when(me - step >= 0)
        def _():
            copy(step).wait_send()


def local(count, query, keys, values, out_attn, dout, docs):
    rows, width = keys.shape
    heads = query.shape[1] // width
    window = (REACH + 1) * rows
    tile = math.gcd(rows, 256)
    bf16, f32 = jnp.bfloat16, jnp.float32
    vmem = pl.BlockSpec(memory_space=pltpu.VMEM)
    anywhere = pl.BlockSpec(memory_space=pltpu.HBM)
    shape = jax.ShapeDtypeStruct
    kaug, k_turned, v_all, doc_all = pl.pallas_call(
        functools.partial(gather_kernel, count),
        out_shape=(
            shape((window, 2 * width), bf16),
            shape((width, window), bf16),
            shape((window, width), bf16),
            shape((REACH + 1, rows), jnp.int32),
        ),
        in_specs=[anywhere, anywhere, vmem],
        out_specs=(vmem,) * 4,
        scratch_shapes=[
            pltpu.VMEM((REACH + 1, rows, width), bf16),
            pltpu.VMEM((REACH + 1, rows, width), bf16),
            pltpu.VMEM((8, rows), jnp.int32),
            pltpu.VMEM((REACH, 8, rows), jnp.int32),
            pltpu.SemaphoreType.DMA((REACH, 3)),
            pltpu.SemaphoreType.DMA((REACH, 3)),
            pltpu.SemaphoreType.DMA((2,)),
        ],
        compiler_params=pltpu.CompilerParams(
            collective_id=0, has_side_effects=True, vmem_limit_bytes=62 << 20
        ),
    )(keys, values, docs.reshape(1, rows))
    dquery, part, own = pl.pallas_call(
        functools.partial(attend_kernel, heads, tile),
        out_shape=(
            shape(query.shape, bf16),
            shape((window - rows, 2 * width), bf16),
            shape((rows, 2 * width), f32),
        ),
        in_specs=[anywhere] * 3 + [vmem] * 4,
        out_specs=(vmem,) * 3,
        scratch_shapes=[
            pltpu.VMEM(query.shape, bf16),
            pltpu.VMEM(query.shape, bf16),
            pltpu.VMEM(query.shape, bf16),
            pltpu.VMEM((heads, window, tile), f32),
            pltpu.VMEM((tile, heads * tile), bf16),
            pltpu.VMEM((tile, heads * tile), bf16),
            pltpu.VMEM((heads, width, tile), f32),
            pltpu.VMEM((heads, 2 * width, tile), bf16),
            pltpu.VMEM((heads, width, tile), bf16),
            pltpu.VMEM((heads * tile, width), bf16),
            pltpu.VMEM((heads * tile, width), bf16),
            pltpu.VMEM((window, width), f32),
            pltpu.VMEM((window, width), f32),
            pltpu.SemaphoreType.DMA((rows // tile, 3)),
        ],
        compiler_params=pltpu.CompilerParams(vmem_limit_bytes=62 << 20),
    )(query, out_attn, dout, kaug, k_turned, v_all, doc_all)
    dkeys, dvalues = pl.pallas_call(
        functools.partial(return_kernel, count),
        out_shape=(shape((rows, width), bf16), shape((rows, width), bf16)),
        in_specs=[anywhere] * 2,
        out_specs=(vmem,) * 2,
        scratch_shapes=[
            pltpu.VMEM((REACH, rows, 2 * width), bf16),
            pltpu.VMEM((rows, 2 * width), f32),
            pltpu.SemaphoreType.DMA((REACH,)),
            pltpu.SemaphoreType.DMA((REACH,)),
            pltpu.SemaphoreType.DMA,
        ],
        compiler_params=pltpu.CompilerParams(
            collective_id=1, has_side_effects=True, vmem_limit_bytes=62 << 20
        ),
    )(part, own)
    return (dquery, dkeys, dvalues)


def solution(mesh):
    rows = P(("groups", "blocks"), None)
    return jax.shard_map(
        functools.partial(local, mesh.shape["blocks"]),
        mesh=mesh,
        in_specs=(rows,) * 5 + (P(("groups", "blocks")),),
        out_specs=(rows,) * 3,
        check_vma=False,
    )
```

```python
import functools
import math

import jax
import jax.numpy as jnp
from jax import lax
from jax.experimental import pallas as pl
from jax.experimental.pallas import tpu as pltpu
from jax.sharding import PartitionSpec as P

REACH = 3
FAR = 2.0**18
MESH = pl.DeviceIdType.MESH
NT = (((1,), (1,)), ((), ()))


def greet_and_count(sources, waits, count):
    barrier = pltpu.get_barrier_semaphore()
    for other in sources:

        @pl.when((other >= 0) & (other < count))
        def _():
            pl.semaphore_signal(
                barrier, inc=1, device_id={"blocks": other}, device_id_type=MESH
            )

    @pl.when(waits > 0)
    def _():
        pl.semaphore_wait(barrier, waits)


def gather_kernel(
    count, k_ref, v_ref, d_ref, kaug_ref, kt_ref, vall_ref, docs_ref,
    k_in, v_in, d_out, d_in, send_sem, recv_sem, own_sem,
):
    me = lax.axis_index("blocks")
    rows = k_ref.shape[0]
    width = k_ref.shape[1]
    bring = [
        pltpu.make_async_copy(src, dst.at[REACH], own_sem.at[i])
        for i, (src, dst) in enumerate(((k_ref, k_in), (v_ref, v_in)))
    ]
    for copy in bring:
        copy.start()
    d_out[...] = jnp.broadcast_to(d_ref[...], d_out.shape)
    greet_and_count(
        [me - step for step in range(1, REACH + 1)],
        jnp.minimum(count - 1 - me, REACH),
        count,
    )

    def copies(step):
        slot = REACH - step
        pairs = ((k_ref, k_in), (v_ref, v_in), (d_out, d_in))
        return [
            pltpu.make_async_remote_copy(
                src_ref=src,
                dst_ref=dst.at[slot],
                send_sem=send_sem.at[slot, i],
                recv_sem=recv_sem.at[slot, i],
                device_id={"blocks": me + step},
                device_id_type=MESH,
            )
            for i, (src, dst) in enumerate(pairs)
        ]

    for step in range(REACH, 0, -1):

        @pl.when(me + step < count)
        def _():
            for copy in copies(step):
                copy.start()

    def place(block, k_rows, v_rows, doc_row):
        hot = lax.broadcasted_iota(jnp.int32, (width, rows), 0) == doc_row
        feature = jnp.transpose(jnp.where(hot, 0.0, -FAR).astype(jnp.float32))
        kaug_ref[pl.ds(block * rows, rows), :width] = k_rows
        kaug_ref[pl.ds(block * rows, rows), width:] = feature.astype(jnp.bfloat16)
        kt_ref[:, pl.ds(block * rows, rows)] = jnp.transpose(k_rows)
        vall_ref[pl.ds(block * rows, rows), :] = v_rows
        docs_ref[block : block + 1, :] = doc_row

    for copy in bring:
        copy.wait()
    place(REACH, k_in[REACH], v_in[REACH], d_ref[...])
    for step in range(1, REACH + 1):
        slot = REACH - step

        @pl.when(me - step >= 0)
        def _():
            for copy in copies(step):
                copy.wait_recv()
            place(slot, k_in[slot], v_in[slot], d_in[slot, :1, :])

        @pl.when(me - step < 0)
        def _():
            zero = jnp.zeros((rows, width), jnp.bfloat16)
            place(slot, zero, zero, jnp.full((1, rows), -1, jnp.int32))

    for step in range(1, REACH + 1):

        @pl.when(me + step < count)
        def _():
            for copy in copies(step):
                copy.wait_send()


def attend_kernel(
    heads, tile,
    q_hbm, o_hbm, g_hbm, kaug_ref, kt_ref, v_ref, docs_ref,
    dq_ref, part_ref, own_ref,
    q_ref, o_ref, g_ref,
    s_scr, p_scr, ds_scr, dqt_scr, qa_scr, gt_scr, qs_scr, gs_scr, dk_scr, dv_scr, sems,
):
    rows = q_ref.shape[0]
    width = v_ref.shape[1]
    window = v_ref.shape[0]
    scale = 1.0 / math.sqrt(width)
    to_two = scale * math.log2(math.e)
    past = window - rows

    def bring(j):
        part = pl.ds(j * tile, tile)
        pairs = ((q_hbm, q_ref), (g_hbm, g_ref), (o_hbm, o_ref))
        return [
            pltpu.make_async_copy(src.at[part, :], dst.at[part, :], sems.at[j, i])
            for i, (src, dst) in enumerate(pairs)
        ]

    for j in range(rows // tile):
        for copy in bring(j):
            copy.start()
    dk_scr[...] = jnp.zeros_like(dk_scr)
    dv_scr[...] = jnp.zeros_like(dv_scr)
    ones = jnp.ones((8, 2 * width), jnp.bfloat16)
    docs = docs_ref[...]
    tri = jnp.where(
        lax.broadcasted_iota(jnp.int32, (tile, tile), 0)
        <= lax.broadcasted_iota(jnp.int32, (tile, tile), 1),
        0.0,
        -FAR,
    ).astype(jnp.float32)

    for j in range(rows // tile):
        own = slice(j * tile, (j + 1) * tile)
        doc_first = docs_ref[REACH : REACH + 1, j * tile : j * tile + 1]
        before = jnp.sum(jnp.where(docs < doc_first, 1.0, 0.0)).astype(jnp.int32)
        first = before // tile
        last = past // tile + j
        hot = lax.broadcasted_iota(jnp.int32, (width, tile), 0) == docs[REACH:, own]
        hot = jnp.where(hot, 1.0, 0.0).astype(jnp.bfloat16)
        for copy in bring(j):
            copy.wait()
        deltas = []
        for h in range(heads):
            cols = slice(h * width, (h + 1) * width)
            qh = q_ref[own, cols]
            gh = g_ref[own, cols]
            qa_scr[h, :width, :] = jnp.transpose(qh)
            qa_scr[h, width:, :] = hot
            gt_scr[h] = jnp.transpose(gh)
            qs_scr[h * tile : (h + 1) * tile, :] = qh
            gs_scr[h * tile : (h + 1) * tile, :] = gh
            both = gh.astype(jnp.float32) * o_ref[own, cols].astype(jnp.float32)
            high = both.astype(jnp.bfloat16)
            less = (both - high.astype(jnp.float32)).astype(jnp.bfloat16)
            deltas.append(
                lax.dot_general(
                    ones, jnp.concatenate([high, less], axis=1), NT,
                    preferred_element_type=jnp.float32,
                )[:1]
            )

        def fold(part, how):
            return how(part.reshape(tile // 8, 8, tile), axis=0)

        def score(c, tops, bias):
            at = pl.ds(pl.multiple_of(c * tile, tile), tile)
            kc = kaug_ref[at, :]
            new = []
            for h in range(heads):
                s = jnp.dot(kc, qa_scr[h], preferred_element_type=jnp.float32)
                if bias is not None:
                    s = s + bias
                s_scr[h, at, :] = s
                new.append(jnp.maximum(tops[h], fold(s, jnp.max)))
            return tuple(new)

        tops = tuple(jnp.full((8, tile), -1e30, jnp.float32) for _ in range(heads))
        tops = lax.fori_loop(first, last, lambda c, t: score(c, t, None), tops)
        tops = score(last, tops, tri)
        tops = [jnp.max(t, axis=0, keepdims=True) for t in tops]

        def expo(c, sums):
            at = pl.ds(pl.multiple_of(c * tile, tile), tile)
            new = []
            for h in range(heads):
                e = jnp.exp2((s_scr[h, at, :] - tops[h]) * to_two)
                s_scr[h, at, :] = e
                new.append(sums[h] + fold(e, jnp.sum))
            return tuple(new)

        sums = tuple(jnp.zeros((8, tile), jnp.float32) for _ in range(heads))
        sums = lax.fori_loop(first, last + 1, expo, sums)
        shares = [1.0 / jnp.sum(t, axis=0, keepdims=True) for t in sums]
        dqt_scr[...] = jnp.zeros_like(dqt_scr)

        def grads(c, carry):
            at = pl.ds(pl.multiple_of(c * tile, tile), tile)
            vc = v_ref[at, :]
            kt = kt_ref[:, at]
            for h in range(heads):
                here = slice(h * tile, (h + 1) * tile)
                gp = jnp.dot(vc, gt_scr[h], preferred_element_type=jnp.float32)
                p = s_scr[h, at, :] * shares[h]
                p_scr[:, here] = p.astype(jnp.bfloat16)
                ds = (p * (gp - deltas[h])).astype(jnp.bfloat16)
                ds_scr[:, here] = ds
            dv_scr[at, :] += jnp.dot(
                p_scr[...], gs_scr[...], preferred_element_type=jnp.float32
            )
            dk_scr[at, :] += jnp.dot(
                ds_scr[...], qs_scr[...], preferred_element_type=jnp.float32
            )
            for h in range(heads):
                here = slice(h * tile, (h + 1) * tile)
                dqt_scr[h] += jnp.dot(
                    kt, ds_scr[:, here], preferred_element_type=jnp.float32
                )
            return carry

        lax.fori_loop(first, last + 1, grads, 0)
        for h in range(heads):
            dq_ref[own, h * width : (h + 1) * width] = jnp.transpose(
                dqt_scr[h] * scale
            ).astype(jnp.bfloat16)

    part_ref[:, :width] = (dk_scr[:past, :] * scale).astype(jnp.bfloat16)
    part_ref[:, width:] = dv_scr[:past, :].astype(jnp.bfloat16)
    own_ref[:, :width] = dk_scr[past:, :] * scale
    own_ref[:, width:] = dv_scr[past:, :]


def return_kernel(
    count, part_ref, own_hbm, dk_ref, dv_ref, held, own_ref, send_sem, recv_sem, own_sem
):
    me = lax.axis_index("blocks")
    bring = pltpu.make_async_copy(own_hbm, own_ref, own_sem)
    bring.start()
    rows, width = dk_ref.shape
    greet_and_count(
        [me + step for step in range(1, REACH + 1)],
        jnp.minimum(me, REACH),
        count,
    )

    def copy(step):
        slot = REACH - step
        return pltpu.make_async_remote_copy(
            src_ref=part_ref.at[pl.ds(slot * rows, rows), :],
            dst_ref=held.at[slot],
            send_sem=send_sem.at[slot],
            recv_sem=recv_sem.at[slot],
            device_id={"blocks": me - step},
            device_id_type=MESH,
        )

    for step in range(REACH, 0, -1):

        @pl.when(me - step >= 0)
        def _():
            copy(step).start()

        @pl.when(me + step >= count)
        def _():
            held[REACH - step] = jnp.zeros(held.shape[1:], held.dtype)

    for step in range(1, REACH + 1):

        @pl.when(me + step < count)
        def _():
            copy(step).wait_recv()

    bring.wait()
    total = own_ref[...]
    for step in range(1, REACH + 1):
        total = total + held[REACH - step].astype(jnp.float32)
    dk_ref[...] = total[:, :width].astype(jnp.bfloat16)
    dv_ref[...] = total[:, width:].astype(jnp.bfloat16)
    for step in range(1, REACH + 1):

        @pl.when(me - step >= 0)
        def _():
            copy(step).wait_send()


def local(count, query, keys, values, out_attn, dout, docs):
    rows, width = keys.shape
    heads = query.shape[1] // width
    window = (REACH + 1) * rows
    tile = math.gcd(rows, 256)
    bf16, f32 = jnp.bfloat16, jnp.float32
    vmem = pl.BlockSpec(memory_space=pltpu.VMEM)
    anywhere = pl.BlockSpec(memory_space=pltpu.HBM)
    shape = jax.ShapeDtypeStruct
    kaug, k_turned, v_all, doc_all = pl.pallas_call(
        functools.partial(gather_kernel, count),
        out_shape=(
            shape((window, 2 * width), bf16),
            shape((width, window), bf16),
            shape((window, width), bf16),
            shape((REACH + 1, rows), jnp.int32),
        ),
        in_specs=[anywhere, anywhere, vmem],
        out_specs=(vmem,) * 4,
        scratch_shapes=[
            pltpu.VMEM((REACH + 1, rows, width), bf16),
            pltpu.VMEM((REACH + 1, rows, width), bf16),
            pltpu.VMEM((8, rows), jnp.int32),
            pltpu.VMEM((REACH, 8, rows), jnp.int32),
            pltpu.SemaphoreType.DMA((REACH, 3)),
            pltpu.SemaphoreType.DMA((REACH, 3)),
            pltpu.SemaphoreType.DMA((2,)),
        ],
        compiler_params=pltpu.CompilerParams(
            collective_id=0, has_side_effects=True, vmem_limit_bytes=62 << 20
        ),
    )(keys, values, docs.reshape(1, rows))
    dquery, part, own = pl.pallas_call(
        functools.partial(attend_kernel, heads, tile),
        out_shape=(
            shape(query.shape, bf16),
            shape((window - rows, 2 * width), bf16),
            shape((rows, 2 * width), f32),
        ),
        in_specs=[anywhere] * 3 + [vmem] * 4,
        out_specs=(vmem,) * 3,
        scratch_shapes=[
            pltpu.VMEM(query.shape, bf16),
            pltpu.VMEM(query.shape, bf16),
            pltpu.VMEM(query.shape, bf16),
            pltpu.VMEM((heads, window, tile), f32),
            pltpu.VMEM((tile, heads * tile), bf16),
            pltpu.VMEM((tile, heads * tile), bf16),
            pltpu.VMEM((heads, width, tile), f32),
            pltpu.VMEM((heads, 2 * width, tile), bf16),
            pltpu.VMEM((heads, width, tile), bf16),
            pltpu.VMEM((heads * tile, width), bf16),
            pltpu.VMEM((heads * tile, width), bf16),
            pltpu.VMEM((window, width), f32),
            pltpu.VMEM((window, width), f32),
            pltpu.SemaphoreType.DMA((rows // tile, 3)),
        ],
        compiler_params=pltpu.CompilerParams(vmem_limit_bytes=62 << 20),
    )(query, out_attn, dout, kaug, k_turned, v_all, doc_all)
    dkeys, dvalues = pl.pallas_call(
        functools.partial(return_kernel, count),
        out_shape=(shape((rows, width), bf16), shape((rows, width), bf16)),
        in_specs=[anywhere] * 2,
        out_specs=(vmem,) * 2,
        scratch_shapes=[
            pltpu.VMEM((REACH, rows, 2 * width), bf16),
            pltpu.VMEM((rows, 2 * width), f32),
            pltpu.SemaphoreType.DMA((REACH,)),
            pltpu.SemaphoreType.DMA((REACH,)),
            pltpu.SemaphoreType.DMA,
        ],
        compiler_params=pltpu.CompilerParams(
            collective_id=1, has_side_effects=True, vmem_limit_bytes=62 << 20
        ),
    )(part, own)
    return (dquery, dkeys, dvalues)


def solution(mesh):
    rows = P(("groups", "blocks"), None)
    return jax.shard_map(
        functools.partial(local, mesh.shape["blocks"]),
        mesh=mesh,
        in_specs=(rows,) * 5 + (P(("groups", "blocks")),),
        out_specs=(rows,) * 3,
        check_vma=False,
    )
```

```python
import functools
import math

import jax
import jax.numpy as jnp
from jax import lax
from jax.experimental import pallas as pl
from jax.experimental.pallas import tpu as pltpu
from jax.sharding import PartitionSpec as P

REACH = 3
FAR = 2.0**18
MESH = pl.DeviceIdType.MESH
NT = (((1,), (1,)), ((), ()))


def greet_and_count(sources, waits, count):
    barrier = pltpu.get_barrier_semaphore()
    for other in sources:

        @pl.when((other >= 0) & (other < count))
        def _():
            pl.semaphore_signal(
                barrier, inc=1, device_id={"blocks": other}, device_id_type=MESH
            )

    @pl.when(waits > 0)
    def _():
        pl.semaphore_wait(barrier, waits)


def gather_kernel(
    count, k_ref, v_ref, d_ref, kaug_ref, kt_ref, vall_ref, docs_ref,
    k_in, v_in, d_out, d_in, send_sem, recv_sem, own_sem,
):
    me = lax.axis_index("blocks")
    rows = k_ref.shape[0]
    width = k_ref.shape[1]
    bring = [
        pltpu.make_async_copy(src, dst.at[REACH], own_sem.at[i])
        for i, (src, dst) in enumerate(((k_ref, k_in), (v_ref, v_in)))
    ]
    for copy in bring:
        copy.start()
    d_out[...] = jnp.broadcast_to(d_ref[...], d_out.shape)
    core = me % 2
    mate = me + 1 - 2 * core
    greet_and_count(
        [me - 2, mate, jnp.where(core == 0, me - 3, -1)],
        1
        + jnp.where(me + 2 < count, 1, 0)
        + jnp.where((core == 1) & (me + 3 < count), 1, 0),
        count,
    )

    def copies(kind, slot, target, handed):
        pairs = ((k_ref, k_in), (v_ref, v_in), (d_out, d_in))
        return [
            pltpu.make_async_remote_copy(
                src_ref=dst.at[1] if handed else src,
                dst_ref=dst.at[slot],
                send_sem=send_sem.at[kind, i],
                recv_sem=recv_sem.at[slot, i],
                device_id={"blocks": target},
                device_id_type=MESH,
            )
            for i, (src, dst) in enumerate(pairs)
        ]

    plans = (
        (me + 2 < count, copies(0, 1, me + 2, False)),
        (core == 0, copies(1, 2, me + 1, False)),
        ((core == 1) & (me + 3 < count), copies(1, 0, me + 3, False)),
        ((core == 0) & (me >= 2), copies(2, 0, mate, True)),
        ((core == 1) & (me >= 2), copies(2, 2, mate, True)),
    )

    def start(plan):
        @pl.when(plan[0])
        def _():
            for copy in plan[1]:
                copy.start()

    for plan in plans[:3]:
        start(plan)

    def place(block, k_rows, v_rows, doc_row):
        hot = lax.broadcasted_iota(jnp.int32, (width, rows), 0) == doc_row
        feature = jnp.transpose(jnp.where(hot, 0.0, -FAR).astype(jnp.float32))
        kaug_ref[pl.ds(block * rows, rows), :width] = k_rows
        kaug_ref[pl.ds(block * rows, rows), width:] = feature.astype(jnp.bfloat16)
        kt_ref[:, pl.ds(block * rows, rows)] = jnp.transpose(k_rows)
        vall_ref[pl.ds(block * rows, rows), :] = v_rows
        docs_ref[block : block + 1, :] = doc_row

    for copy in bring:
        copy.wait()
    place(REACH, k_in[REACH], v_in[REACH], d_ref[...])
    for step in (2, 1, 3):
        slot = REACH - step

        @pl.when(me - step >= 0)
        def _():
            for copy in copies(0, slot, mate, False):
                copy.wait_recv()

        if step == 2:
            start(plans[3])
            start(plans[4])

        @pl.when(me - step >= 0)
        def _():
            place(slot, k_in[slot], v_in[slot], d_in[slot, :1, :])

        @pl.when(me - step < 0)
        def _():
            zero = jnp.zeros((rows, width), jnp.bfloat16)
            place(slot, zero, zero, jnp.full((1, rows), -1, jnp.int32))

    for plan in plans:

        @pl.when(plan[0])
        def _():
            for copy in plan[1]:
                copy.wait_send()


def attend_kernel(
    heads, tile,
    q_hbm, o_hbm, g_hbm, kaug_ref, kt_ref, v_ref, docs_ref,
    dq_ref, part_ref, own_ref,
    q_ref, o_ref, g_ref,
    s_scr, p_scr, ds_scr, dqt_scr, qa_scr, gt_scr, qs_scr, gs_scr, dk_scr, dv_scr, sems,
):
    rows = q_ref.shape[0]
    width = v_ref.shape[1]
    window = v_ref.shape[0]
    scale = 1.0 / math.sqrt(width)
    to_two = scale * math.log2(math.e)
    past = window - rows

    def bring(j):
        part = pl.ds(j * tile, tile)
        pairs = ((q_hbm, q_ref), (g_hbm, g_ref), (o_hbm, o_ref))
        return [
            pltpu.make_async_copy(src.at[part, :], dst.at[part, :], sems.at[j, i])
            for i, (src, dst) in enumerate(pairs)
        ]

    for j in range(rows // tile):
        for copy in bring(j):
            copy.start()
    dk_scr[...] = jnp.zeros_like(dk_scr)
    dv_scr[...] = jnp.zeros_like(dv_scr)
    ones = jnp.ones((8, 2 * width), jnp.bfloat16)
    docs = docs_ref[...]
    tri = jnp.where(
        lax.broadcasted_iota(jnp.int32, (tile, tile), 0)
        <= lax.broadcasted_iota(jnp.int32, (tile, tile), 1),
        0.0,
        -FAR,
    ).astype(jnp.float32)

    for j in range(rows // tile):
        own = slice(j * tile, (j + 1) * tile)
        doc_first = docs_ref[REACH : REACH + 1, j * tile : j * tile + 1]
        before = jnp.sum(jnp.where(docs < doc_first, 1.0, 0.0)).astype(jnp.int32)
        first = before // tile
        last = past // tile + j
        hot = lax.broadcasted_iota(jnp.int32, (width, tile), 0) == docs[REACH:, own]
        hot = jnp.where(hot, 1.0, 0.0).astype(jnp.bfloat16)
        for copy in bring(j):
            copy.wait()
        deltas = []
        for h in range(heads):
            cols = slice(h * width, (h + 1) * width)
            qh = q_ref[own, cols]
            gh = g_ref[own, cols]
            qa_scr[h, :width, :] = jnp.transpose(qh)
            qa_scr[h, width:, :] = hot
            gt_scr[h] = jnp.transpose(gh)
            qs_scr[h * tile : (h + 1) * tile, :] = qh
            gs_scr[h * tile : (h + 1) * tile, :] = gh
            both = gh.astype(jnp.float32) * o_ref[own, cols].astype(jnp.float32)
            high = both.astype(jnp.bfloat16)
            less = (both - high.astype(jnp.float32)).astype(jnp.bfloat16)
            deltas.append(
                lax.dot_general(
                    ones, jnp.concatenate([high, less], axis=1), NT,
                    preferred_element_type=jnp.float32,
                )[:1]
            )

        def fold(part, how):
            return how(part.reshape(tile // 8, 8, tile), axis=0)

        def score(c, tops, bias):
            at = pl.ds(pl.multiple_of(c * tile, tile), tile)
            kc = kaug_ref[at, :]
            new = []
            for h in range(heads):
                s = jnp.dot(kc, qa_scr[h], preferred_element_type=jnp.float32)
                if bias is not None:
                    s = s + bias
                s_scr[h, at, :] = s
                new.append(jnp.maximum(tops[h], fold(s, jnp.max)))
            return tuple(new)

        tops = tuple(jnp.full((8, tile), -1e30, jnp.float32) for _ in range(heads))
        tops = lax.fori_loop(first, last, lambda c, t: score(c, t, None), tops)
        tops = score(last, tops, tri)
        tops = [jnp.max(t, axis=0, keepdims=True) for t in tops]

        def expo(c, sums):
            at = pl.ds(pl.multiple_of(c * tile, tile), tile)
            new = []
            for h in range(heads):
                e = jnp.exp2((s_scr[h, at, :] - tops[h]) * to_two)
                s_scr[h, at, :] = e
                new.append(sums[h] + fold(e, jnp.sum))
            return tuple(new)

        sums = tuple(jnp.zeros((8, tile), jnp.float32) for _ in range(heads))
        sums = lax.fori_loop(first, last + 1, expo, sums)
        shares = [1.0 / jnp.sum(t, axis=0, keepdims=True) for t in sums]
        dqt_scr[...] = jnp.zeros_like(dqt_scr)

        def grads(c, carry):
            at = pl.ds(pl.multiple_of(c * tile, tile), tile)
            vc = v_ref[at, :]
            kt = kt_ref[:, at]
            for h in range(heads):
                here = slice(h * tile, (h + 1) * tile)
                gp = jnp.dot(vc, gt_scr[h], preferred_element_type=jnp.float32)
                p = s_scr[h, at, :] * shares[h]
                p_scr[:, here] = p.astype(jnp.bfloat16)
                ds = (p * (gp - deltas[h])).astype(jnp.bfloat16)
                ds_scr[:, here] = ds
            dv_scr[at, :] += jnp.dot(
                p_scr[...], gs_scr[...], preferred_element_type=jnp.float32
            )
            dk_scr[at, :] += jnp.dot(
                ds_scr[...], qs_scr[...], preferred_element_type=jnp.float32
            )
            for h in range(heads):
                here = slice(h * tile, (h + 1) * tile)
                dqt_scr[h] += jnp.dot(
                    kt, ds_scr[:, here], preferred_element_type=jnp.float32
                )
            return carry

        lax.fori_loop(first, last + 1, grads, 0)
        for h in range(heads):
            dq_ref[own, h * width : (h + 1) * width] = jnp.transpose(
                dqt_scr[h] * scale
            ).astype(jnp.bfloat16)

    part_ref[:, :width] = (dk_scr[:past, :] * scale).astype(jnp.bfloat16)
    part_ref[:, width:] = dv_scr[:past, :].astype(jnp.bfloat16)
    own_ref[:, :width] = dk_scr[past:, :] * scale
    own_ref[:, width:] = dv_scr[past:, :]


def return_kernel(
    count, part_ref, own_hbm, dk_ref, dv_ref, held, own_ref, send_sem, recv_sem, own_sem
):
    me = lax.axis_index("blocks")
    bring = pltpu.make_async_copy(own_hbm, own_ref, own_sem)
    bring.start()
    rows, width = dk_ref.shape
    greet_and_count(
        [me + step for step in range(1, REACH + 1)],
        jnp.minimum(me, REACH),
        count,
    )

    def copy(step):
        slot = REACH - step
        return pltpu.make_async_remote_copy(
            src_ref=part_ref.at[pl.ds(slot * rows, rows), :],
            dst_ref=held.at[slot],
            send_sem=send_sem.at[slot],
            recv_sem=recv_sem.at[slot],
            device_id={"blocks": me - step},
            device_id_type=MESH,
        )

    for step in range(REACH, 0, -1):

        @pl.when(me - step >= 0)
        def _():
            copy(step).start()

        @pl.when(me + step >= count)
        def _():
            held[REACH - step] = jnp.zeros(held.shape[1:], held.dtype)

    for step in range(1, REACH + 1):

        @pl.when(me + step < count)
        def _():
            copy(step).wait_recv()

    bring.wait()
    total = own_ref[...]
    for step in range(1, REACH + 1):
        total = total + held[REACH - step].astype(jnp.float32)
    dk_ref[...] = total[:, :width].astype(jnp.bfloat16)
    dv_ref[...] = total[:, width:].astype(jnp.bfloat16)
    for step in range(1, REACH + 1):

        @pl.when(me - step >= 0)
        def _():
            copy(step).wait_send()


def local(count, query, keys, values, out_attn, dout, docs):
    rows, width = keys.shape
    heads = query.shape[1] // width
    window = (REACH + 1) * rows
    tile = math.gcd(rows, 256)
    bf16, f32 = jnp.bfloat16, jnp.float32
    vmem = pl.BlockSpec(memory_space=pltpu.VMEM)
    anywhere = pl.BlockSpec(memory_space=pltpu.HBM)
    shape = jax.ShapeDtypeStruct
    kaug, k_turned, v_all, doc_all = pl.pallas_call(
        functools.partial(gather_kernel, count),
        out_shape=(
            shape((window, 2 * width), bf16),
            shape((width, window), bf16),
            shape((window, width), bf16),
            shape((REACH + 1, rows), jnp.int32),
        ),
        in_specs=[anywhere, anywhere, vmem],
        out_specs=(vmem,) * 4,
        scratch_shapes=[
            pltpu.VMEM((REACH + 1, rows, width), bf16),
            pltpu.VMEM((REACH + 1, rows, width), bf16),
            pltpu.VMEM((8, rows), jnp.int32),
            pltpu.VMEM((REACH, 8, rows), jnp.int32),
            pltpu.SemaphoreType.DMA((REACH, 3)),
            pltpu.SemaphoreType.DMA((REACH, 3)),
            pltpu.SemaphoreType.DMA((2,)),
        ],
        compiler_params=pltpu.CompilerParams(
            collective_id=0, has_side_effects=True, vmem_limit_bytes=62 << 20
        ),
    )(keys, values, docs.reshape(1, rows))
    dquery, part, own = pl.pallas_call(
        functools.partial(attend_kernel, heads, tile),
        out_shape=(
            shape(query.shape, bf16),
            shape((window - rows, 2 * width), bf16),
            shape((rows, 2 * width), f32),
        ),
        in_specs=[anywhere] * 3 + [vmem] * 4,
        out_specs=(vmem,) * 3,
        scratch_shapes=[
            pltpu.VMEM(query.shape, bf16),
            pltpu.VMEM(query.shape, bf16),
            pltpu.VMEM(query.shape, bf16),
            pltpu.VMEM((heads, window, tile), f32),
            pltpu.VMEM((tile, heads * tile), bf16),
            pltpu.VMEM((tile, heads * tile), bf16),
            pltpu.VMEM((heads, width, tile), f32),
            pltpu.VMEM((heads, 2 * width, tile), bf16),
            pltpu.VMEM((heads, width, tile), bf16),
            pltpu.VMEM((heads * tile, width), bf16),
            pltpu.VMEM((heads * tile, width), bf16),
            pltpu.VMEM((window, width), f32),
            pltpu.VMEM((window, width), f32),
            pltpu.SemaphoreType.DMA((rows // tile, 3)),
        ],
        compiler_params=pltpu.CompilerParams(vmem_limit_bytes=62 << 20),
    )(query, out_attn, dout, kaug, k_turned, v_all, doc_all)
    dkeys, dvalues = pl.pallas_call(
        functools.partial(return_kernel, count),
        out_shape=(shape((rows, width), bf16), shape((rows, width), bf16)),
        in_specs=[anywhere] * 2,
        out_specs=(vmem,) * 2,
        scratch_shapes=[
            pltpu.VMEM((REACH, rows, 2 * width), bf16),
            pltpu.VMEM((rows, 2 * width), f32),
            pltpu.SemaphoreType.DMA((REACH,)),
            pltpu.SemaphoreType.DMA((REACH,)),
            pltpu.SemaphoreType.DMA,
        ],
        compiler_params=pltpu.CompilerParams(
            collective_id=1, has_side_effects=True, vmem_limit_bytes=62 << 20
        ),
    )(part, own)
    return (dquery, dkeys, dvalues)


def solution(mesh):
    rows = P(("groups", "blocks"), None)
    return jax.shard_map(
        functools.partial(local, mesh.shape["blocks"]),
        mesh=mesh,
        in_specs=(rows,) * 5 + (P(("groups", "blocks")),),
        out_specs=(rows,) * 3,
        check_vma=False,
    )
```
